32 devices in a mesh: ens: 2 (over y), lon: 16 (over z, x, core).
Axes of the slice: x: 2, y: 2, z: 4, core: 2. Of those that a mesh axis runs over, the one named last changes fastest.
Arguments:
- saved_input: bfloat16 [32, 192, 16, 128], P(('ens', 'lon')), parts along dimension 0, may hold values from -127 to 127, as said below
- tile_scale: float32 [32, 8, 192], P(('ens', 'lon')), parts along dimension 0, may hold values from 0.002 to 0.03
- ocean_tiles: int32 [32, 8], P(('ens', 'lon')), parts along dimension 0, may hold values from 0 to 1, as said below
- upstream: bfloat16 [32, 192, 16, 128], P(('ens', 'lon')), parts along dimension 0, may hold values from -6 to 6
- kernel: float32 [49, 192], replicated, may hold values from -0.875 to 0.875
- kernel_offset: float32 [192], replicated, may hold values from -3 to 3
- norm_gain: float32 [192], replicated, may hold values from 0.5 to 2
- norm_shift: float32 [192], replicated, may hold values from -3 to 3
- lift_weight: bfloat16 [192, 768], replicated, may hold values from -0.4375 to 0.4375
- lift_bias: float32 [768], replicated, may hold values from -3 to 3
- drop_weight: bfloat16 [768, 192], replicated, may hold values from -0.21875 to 0.21875
Outputs:
- grad_input: bfloat16 [32, 192, 16, 128], P(('ens', 'lon')), parts along dimension 0
- grad_kernel: float32 [98, 192], P('ens'), parts along dimension 0
- grad_offset: float32 [384], P('ens'), parts along dimension 0
- grad_gain: float32 [384], P('ens'), parts along dimension 0
- grad_shift: float32 [384], P('ens'), parts along dimension 0
- grad_lift: float32 [384, 768], P('ens'), parts along dimension 0
- grad_bias: float32 [1536], P('ens'), parts along dimension 0
- grad_drop: float32 [1536, 192], P('ens'), parts along dimension 0
The draws below stay inside these ranges and needn't reach their ends.
There are 2 independent parts, one for each index of `ens`. The reference program is written for one: setup_inputs(seed, part) draws one part's arguments, and reference() takes and returns one part's arrays. A program takes and returns all parts, laid end to end along the dimension named above; an argument that names none is the same for every part. Nothing has to cross between parts.
Inputs may be any that keep to these rules, and one draw needn't show every extreme that they name: `saved_input`: whole numbers. `ocean_tiles`: some block holds no ocean tile.
All inputs are finite; a program needn't handle non-finite values.
Results may differ from the reference program's by a relative error of at most 0.0068.
Values may be sent and summed in bfloat16 or wider, within the bound.
A program may use at most 64 MiB of HBM per device.

```python
import math
import jax
import jax.numpy as jnp
from jax import lax

C = 192
H = 768
KS = 7
TL = 16
SLOTS = 8
LAT_DEVS = 8
BLOCKS = 16
NLAT = 128
NLON = 256
NCELLS = 32768
N_LON = 16


def draw_saved_input(key, part):
    key = jax.random.fold_in(key, 11)
    levels = jax.random.randint(key, (BLOCKS, C, TL, SLOTS * TL), -127, 128)
    return levels.astype(jnp.bfloat16)


def draw_ocean_tiles(key, part):
    key = jax.random.fold_in(key, 5)
    key_counts, key_col, key_row, key_place = jax.random.split(key, 4)
    block_ids = jnp.arange(BLOCKS, dtype=jnp.int32)
    places = (block_ids + 1) % BLOCKS
    rows = places % LAT_DEVS
    counts = jax.random.randint(key_counts, (BLOCKS,), 0, SLOTS + 1)
    counts = jnp.where(rows < LAT_DEVS // 2, SLOTS, counts)
    forced_col = jax.random.randint(key_col, (), 0, BLOCKS // LAT_DEVS)
    forced_row = LAT_DEVS // 2 + jax.random.randint(key_row, (), 0, LAT_DEVS - LAT_DEVS // 2)
    forced_place = forced_col * LAT_DEVS + forced_row
    counts = jnp.where(places == forced_place, 0, counts)
    scores = jax.random.randint(key_place, (BLOCKS, SLOTS), 0, 1 << 20) * SLOTS + jnp.arange(SLOTS)[None, :]
    ranks = jnp.argsort(jnp.argsort(scores, axis=1), axis=1)
    return (ranks < counts[:, None]).astype(jnp.int32)


def block_scale(own_key, dims, cuts, smallest, top_value):
    def one(position, blocks):
        heights = jax.random.uniform(jax.random.fold_in(jax.random.fold_in(own_key, 6), position), (blocks,), jnp.float32, smallest / len(cuts), top_value / len(cuts))
        return jnp.repeat(jnp.exp(heights), dims[position] // blocks).reshape((-1,) + (1,) * (len(dims) - position - 1))

    gain = one(*cuts[0])
    for cut in cuts[1:]:
        gain = gain * one(*cut)
    return gain


def bell_draw(stream_key, dims, width, most, cuts=(), kind=jnp.bfloat16):
    drawn = jax.random.normal(stream_key, dims, jnp.float32) * width
    if len(cuts) > 0:
        drawn = block_scale(stream_key, dims, cuts, -0.22, 0.18) * drawn
    return jnp.clip(drawn, min=-most, max=most).astype(kind)


def setup_inputs(seed: int = 0, part: int = 0) -> dict:
    streams_of = jax.random.split(jax.random.key(seed), 12)
    part_keys = jax.random.split(jax.random.fold_in(streams_of[11], part), 12)
    saved_input = draw_saved_input(jax.random.fold_in(jax.random.fold_in(streams_of[11], part), 71), part)
    tile_scale = jnp.clip(jnp.exp(math.log(0.03) - 2.70805 * jax.random.uniform(part_keys[1], (BLOCKS, SLOTS, C), jnp.float32) ** block_scale(part_keys[1], (BLOCKS, SLOTS, C), ((0, 16),), -0.2, 0.2)), 0.002, 0.03)
    ocean_tiles = draw_ocean_tiles(jax.random.fold_in(jax.random.fold_in(streams_of[11], part), 71), part)
    upstream = bell_draw(part_keys[3], (BLOCKS, C, TL, SLOTS * TL), 1.0, 6.0, ((0, 16),))
    kernel = bell_draw(streams_of[4], (KS * KS, C), (KS * KS) ** -0.5, 0.875, (), jnp.float32)
    kernel_offset = bell_draw(streams_of[5], (C,), 0.5, 3.0, (), jnp.float32)
    norm_gain = jnp.clip(jnp.exp(jax.random.uniform(streams_of[6], (C,), jnp.float32, math.log(0.5), math.log(2.0))), 0.5, 2.0)
    norm_shift = bell_draw(streams_of[7], (C,), 0.5, 3.0, (), jnp.float32)
    lift_weight = bell_draw(streams_of[8], (C, H), C ** -0.5, 0.4375)
    lift_bias = bell_draw(streams_of[9], (H,), 0.5, 3.0, (), jnp.float32)
    drop_weight = bell_draw(streams_of[10], (H, C), H ** -0.5, 0.21875)
    return {"saved_input": saved_input, "tile_scale": tile_scale, "ocean_tiles": ocean_tiles, "upstream": upstream, "kernel": kernel, "kernel_offset": kernel_offset, "norm_gain": norm_gain, "norm_shift": norm_shift, "lift_weight": lift_weight, "lift_bias": lift_bias, "drop_weight": drop_weight}


EPSILON = 1e-06

def gelu_tanh(value):
    return jax.nn.gelu(value, approximate=True)

def depthwise(padded, kernel, offset, tile_rows, block_cols, span):
    total = jnp.zeros((padded.shape[0], tile_rows, block_cols), jnp.float32) + offset[:, None, None]
    for tap_row in range(span):
        for tap_col in range(span):
            weight = kernel[tap_row * span + tap_col][:, None, None]
            total = total + weight * padded[:, tap_row:tap_row + tile_rows, tap_col:tap_col + block_cols].astype(jnp.float32)
    return total

def mlp_backward(pre_norm, cotangent, norm_gain, norm_shift, lift_weight, lift_bias, drop_weight):
    centre = pre_norm - lax.optimization_barrier(jnp.mean(pre_norm, axis=0, keepdims=True))
    inverse = lax.rsqrt(lax.optimization_barrier(jnp.mean(centre * centre, axis=0, keepdims=True)) + EPSILON)
    normed = centre * inverse
    lifted = (normed * norm_gain[:, None] + norm_shift[:, None]).astype(jnp.bfloat16)
    hidden = jnp.dot(lift_weight.T, lifted, preferred_element_type=jnp.float32) + lift_bias[:, None]
    activated, gelu_back = jax.vjp(gelu_tanh, hidden)
    activated = activated.astype(jnp.bfloat16)
    drop_grad = jnp.dot(activated, cotangent.T, preferred_element_type=jnp.float32)
    act_grad = jnp.dot(drop_weight, cotangent, preferred_element_type=jnp.float32)
    hidden_grad = gelu_back(act_grad)[0]
    bias_grad = lax.optimization_barrier(jnp.sum(hidden_grad, axis=1))
    hidden_round = hidden_grad.astype(jnp.bfloat16)
    lift_grad = jnp.dot(lifted, hidden_round.T, preferred_element_type=jnp.float32)
    lifted_grad = jnp.dot(lift_weight, hidden_round, preferred_element_type=jnp.float32)
    gain_grad = lax.optimization_barrier(jnp.sum(lifted_grad * normed, axis=1))
    shift_grad = lax.optimization_barrier(jnp.sum(lifted_grad, axis=1))
    normed_grad = lifted_grad * norm_gain[:, None]
    pre_grad = inverse * (normed_grad - lax.optimization_barrier(jnp.mean(normed_grad, axis=0, keepdims=True)) - normed * lax.optimization_barrier(jnp.mean(normed_grad * normed, axis=0, keepdims=True)))
    return (pre_grad.astype(jnp.bfloat16), (lift_grad, drop_grad, bias_grad, gain_grad, shift_grad))

def conv_backward(padded_x, padded_d, kernel, tile_rows, block_cols, span):
    reach = span // 2
    pre_grad = padded_d[:, reach:reach + tile_rows, reach:reach + block_cols].astype(jnp.float32)
    kernel_terms = []
    input_grad = jnp.zeros((padded_x.shape[0], tile_rows, block_cols), jnp.float32)
    for tap_row in range(span):
        for tap_col in range(span):
            window = padded_x[:, tap_row:tap_row + tile_rows, tap_col:tap_col + block_cols].astype(jnp.float32)
            kernel_terms.append(lax.optimization_barrier(jnp.sum(pre_grad * window, axis=(1, 2))))
            flipped = padded_d[:, 2 * reach - tap_row:2 * reach - tap_row + tile_rows, 2 * reach - tap_col:2 * reach - tap_col + block_cols].astype(jnp.float32)
            input_grad = input_grad + kernel[tap_row * span + tap_col][:, None, None] * flipped
    return (jnp.stack(kernel_terms), lax.optimization_barrier(jnp.sum(pre_grad, axis=(1, 2))), input_grad)

def reference(saved_input, tile_scale, ocean_tiles, upstream, kernel, kernel_offset, norm_gain, norm_shift, lift_weight, lift_bias, drop_weight):
    reach = KS // 2
    block_cols = SLOTS * TL
    columns = N_LON // LAT_DEVS
    mask_cells = jnp.repeat(ocean_tiles, TL, axis=1).astype(jnp.float32)
    scale_cells = jnp.repeat(jnp.transpose(tile_scale, (0, 2, 1)), TL, axis=2)
    field = (saved_input.astype(jnp.float32) * scale_cells[:, :, None, :] * mask_cells[:, None, None, :]).astype(jnp.bfloat16)
    cotangent = upstream * mask_cells[:, None, None, :].astype(jnp.bfloat16)

    def to_grid(blocks):
        by_place = jnp.roll(blocks, 1, axis=0)
        shaped = by_place.reshape(columns, LAT_DEVS, C, TL, block_cols)
        return jnp.transpose(shaped, (2, 1, 3, 0, 4)).reshape(C, NLAT, NLON)

    def pad_grid(grid):
        wrapped = jnp.concatenate([grid[:, :, NLON - reach:], grid, grid[:, :, :reach]], axis=2)
        return jnp.pad(wrapped, ((0, 0), (reach, reach), (0, 0)))

    def window(padded, block_index):
        place = (block_index + 1) % N_LON
        row_start = place % LAT_DEVS * TL
        col_start = place // LAT_DEVS * block_cols
        starts = (jnp.zeros((), jnp.int32), row_start.astype(jnp.int32), col_start.astype(jnp.int32))
        return lax.dynamic_slice(padded, starts, (C, TL + 2 * reach, block_cols + 2 * reach))
    padded_x = pad_grid(to_grid(field))
    zero_grads = (jnp.zeros((C, H), jnp.float32), jnp.zeros((H, C), jnp.float32), jnp.zeros((H,), jnp.float32), jnp.zeros((C,), jnp.float32), jnp.zeros((C,), jnp.float32))

    def first_pass(carry, block_index):
        pre_norm = depthwise(window(padded_x, block_index), kernel, kernel_offset, TL, block_cols, KS)
        pre_grad, grads = mlp_backward(pre_norm.reshape(C, TL * block_cols), cotangent[block_index].reshape(C, TL * block_cols), norm_gain, norm_shift, lift_weight, lift_bias, drop_weight)
        return (jax.tree.map(jnp.add, carry, grads), pre_grad.reshape(C, TL, block_cols))
    block_ids = jnp.arange(N_LON, dtype=jnp.int32)
    grads, grad_blocks = lax.scan(first_pass, zero_grads, block_ids)
    padded_d = pad_grid(to_grid(grad_blocks))

    def second_pass(carry, block_index):
        kernel_term, offset_term, conv_grad = conv_backward(window(padded_x, block_index), window(padded_d, block_index), kernel, TL, block_cols, KS)
        block_grad = (mask_cells[block_index][None, None, :] * (cotangent[block_index].astype(jnp.float32) + conv_grad)).astype(jnp.bfloat16)
        return ((carry[0] + kernel_term, carry[1] + offset_term), block_grad)
    zero_conv = (jnp.zeros((KS * KS, C), jnp.float32), jnp.zeros((C,), jnp.float32))
    conv_sums, grad_input = lax.scan(second_pass, zero_conv, block_ids)
    factor = 1.0 / math.sqrt(NCELLS)
    lift_grad, drop_grad, bias_grad, gain_grad, shift_grad = grads
    return (grad_input, conv_sums[0] * factor, conv_sums[1] * factor, gain_grad * factor, shift_grad * factor, lift_grad * factor, bias_grad * factor, drop_grad * factor)
```

```python
import functools
import math

import jax
import jax.numpy as jnp
from jax import lax
from jax.experimental import pallas as pl
from jax.experimental.pallas import tpu as pltpu
from jax.sharding import PartitionSpec as P

LAT_DEVS = 8
EPSILON = 1e-06
MESH = pl.DeviceIdType.MESH
F32 = jnp.float32
BF16 = jnp.bfloat16


def lanes(shape):
    return lax.broadcasted_iota(jnp.int32, shape, len(shape) - 1)


def roll(x, shift):
    shift = shift % x.shape[-1]
    return x if shift == 0 else pltpu.roll(x, shift, x.ndim - 1)


class Dims:
    def __init__(self, n, channels, rows, cols, span, hidden):
        self.n, self.c, self.rows, self.cols, self.hidden = n, channels, rows, cols, hidden
        self.span, self.reach = span, span // 2
        self.ext = rows + 2 * self.reach
        self.same = 2 * LAT_DEVS == n


def neighbours(d):
    me = lax.axis_index("lon")
    north = lax.rem(me + d.n - 1, d.n)
    south = lax.rem(me + 1, d.n)
    east = lax.rem(me + LAT_DEVS, d.n)
    west = lax.rem(me + d.n - LAT_DEVS, d.n)
    return me, north, south, east, west


def pack_sides(d, main):
    k, r3 = d.reach, d.rows * d.reach

    def step(g, _):
        at = pl.ds(pl.multiple_of(g * 16, 16), 16)
        lane = lanes((16, d.cols))
        packed = jnp.zeros((16, d.cols), F32)
        for r in range(d.rows):
            x = main[r + k, at, :]
            lo, hi = r * k, r3 + r * k
            packed = jnp.where((lane >= lo) & (lane < lo + k), roll(x, lo), packed)
            packed = jnp.where((lane >= hi) & (lane < hi + k), roll(x, hi - (d.cols - k)), packed)
        return at, packed

    return step


def exchange(d, main, side, rows_out, rows_in, pack_out, pack_in, fwd_in, ssem, rsem):
    k = d.reach
    me, north, south, east, west = neighbours(d)

    def copy(src, dst, slot, peer):
        return pltpu.make_async_remote_copy(
            src_ref=src,
            dst_ref=dst,
            send_sem=ssem.at[slot],
            recv_sem=rsem.at[slot],
            device_id={"lon": peer},
            device_id_type=MESH,
        )

    for r in range(k):
        rows_out[0, r] = main[k + r].astype(BF16)
        rows_out[1, r] = main[d.rows + r].astype(BF16)
    to_north = copy(rows_out.at[0], rows_in.at[1], 0, north)
    to_south = copy(rows_out.at[1], rows_in.at[0], 1, south)
    to_north.start()
    to_south.start()
    build = pack_sides(d, main)

    def pack_step(g, carry):
        at, packed = build(g, None)
        pack_out[at, :] = packed.astype(BF16)
        return carry

    lax.fori_loop(0, d.c // 16, pack_step, 0)
    count = 1 if d.same else 2
    sides = [copy(pack_out, pack_in.at[0], 2, west)]
    if not d.same:
        sides.append(copy(pack_out, pack_in.at[1], 3, east))
    for one in sides:
        one.start()

    def finish():
        for one in sides:
            one.wait()
        forwards = []
        for j in range(count):
            forwards.append(copy(pack_in.at[j], fwd_in.at[0, j], 4 + j, south))
            forwards.append(copy(pack_in.at[j], fwd_in.at[1, j], 6 + j, north))
        for one in forwards:
            one.start()
        place = lax.rem(me + 1, LAT_DEVS)
        keep_lower = jnp.where(place != 0, 1.0, 0.0).astype(F32)
        keep_upper = jnp.where(place != LAT_DEVS - 1, 1.0, 0.0).astype(F32)
        r3 = d.rows * k
        last = count - 1

        def unpack(east_pack, west_pack, r):
            lane = lanes(east_pack.shape)
            right = roll(east_pack, -(r * k))
            left = roll(west_pack, (d.cols - k) - (r3 + r * k))
            return jnp.where(lane < d.cols // 2, right, left)

        def own_step(g, carry):
            at = pl.ds(pl.multiple_of(g * 16, 16), 16)
            e, w = pack_in[0, at, :].astype(F32), pack_in[last, at, :].astype(F32)
            for r in range(d.rows):
                side[k + r, at, :] = unpack(e, w, r)
            return carry

        lax.fori_loop(0, d.c // 16, own_step, 0)
        to_north.wait()
        to_south.wait()
        for r in range(k):
            main[r] = rows_in[0, r].astype(F32) * keep_lower
            main[k + d.rows + r] = rows_in[1, r].astype(F32) * keep_upper
        for one in forwards:
            one.wait()

        def corner_step(g, carry):
            at = pl.ds(pl.multiple_of(g * 16, 16), 16)
            ne, nw = fwd_in[0, 0, at, :].astype(F32), fwd_in[0, last, at, :].astype(F32)
            se, sw = fwd_in[1, 0, at, :].astype(F32), fwd_in[1, last, at, :].astype(F32)
            for r in range(k):
                side[r, at, :] = unpack(ne, nw, d.rows - k + r) * keep_lower
                side[k + d.rows + r, at, :] = unpack(se, sw, r) * keep_upper
            return carry

        lax.fori_loop(0, d.c // 16, corner_step, 0)

    return finish


def shifted(d, main, side, at, q):
    s = q - d.reach
    x = main[:, at, :]
    if s == 0:
        return x
    lane = lanes(x.shape)
    h = side[:, at, :]
    keep = lane < s if s > 0 else lane >= d.cols + s
    return roll(jnp.where(keep, h, x), -s)


def depthwise(d, main, side, taps, flip, start, store):
    def group(g, carry):
        at = pl.ds(pl.multiple_of(g * 8, 8), 8)
        weights = taps[at, :]
        acc = start(g, at)
        for q in range(d.span):
            xq = shifted(d, main, side, at, q)
            for p in range(d.span):
                t = p * d.span + q
                if flip:
                    t = d.span * d.span - 1 - t
                acc = acc + weights[:, t : t + 1][None] * xq[p : p + d.rows]
        store(g, at, acc)
        return carry

    lax.fori_loop(0, d.c // 8, group, 0)


def kernel_grads(d, main, side, dmain, small):
    def group(g, carry):
        at = pl.ds(pl.multiple_of(g * 8, 8), 8)
        grad = dmain[d.reach : d.reach + d.rows, at, :]
        lane = lanes((8, d.cols))
        out = small[at, :]
        total = jnp.sum(jnp.sum(grad, axis=0), axis=1, keepdims=True)
        out = jnp.where(lane == d.span * d.span, total, out)
        for q in range(d.span):
            xq = shifted(d, main, side, at, q)
            for p in range(d.span):
                term = jnp.sum(grad * xq[p : p + d.rows], axis=0)
                total = jnp.sum(term, axis=1, keepdims=True)
                out = jnp.where(lane == p * d.span + q, total, out)
        small[at, :] = out
        return carry

    lax.fori_loop(0, d.c // 8, group, 0)


def dot(a, b, dims=((1,), (0,))):
    return lax.dot_general(a, b, (dims, ((), ())), preferred_element_type=F32)


def mlp(d, pre, cot, gain, shift, lift_t, lift, bias, drop, dmain, big_lift, big_drop, gain_acc, shift_acc):
    step_rows = 4
    block = 256
    wide = step_rows * d.cols
    root = math.sqrt(2.0 / math.pi)
    big_lift[...] = jnp.zeros_like(big_lift)
    big_drop[...] = jnp.zeros_like(big_drop)
    gain_acc[...] = jnp.zeros_like(gain_acc)
    shift_acc[...] = jnp.zeros_like(shift_acc)

    def fold(x):
        return sum(x[:, j * d.cols : (j + 1) * d.cols] for j in range(step_rows))

    def step(i, carry):
        r0 = i * step_rows
        x = jnp.concatenate([pre[r0 + j] for j in range(step_rows)], axis=1)
        ct = jnp.concatenate([cot[r0 + j] for j in range(step_rows)], axis=1)
        centre = x - jnp.mean(x, axis=0, keepdims=True)
        inverse = lax.rsqrt(jnp.mean(centre * centre, axis=0, keepdims=True) + EPSILON)
        normed = centre * inverse
        lifted = (normed * gain[...] + shift[...]).astype(BF16)
        ones = jnp.where(
            lax.broadcasted_iota(jnp.int32, (64, wide), 0) == 0, 1.0, 0.0
        ).astype(BF16)
        lifted_one = jnp.concatenate([lifted, ones], axis=0)
        lifted_grad = jnp.zeros((d.c, wide), F32)
        for b in range(d.hidden // block):
            hs = slice(b * block, (b + 1) * block)
            v = dot(lift_t[hs, :], lifted) + bias[hs, :]
            act_grad = dot(drop[hs, :], ct)
            v2 = v * v
            half = 0.5 * jnp.tanh(v * (root + (root * 0.044715) * v2)) + 0.5
            act = v * half
            slope = half + (act * (1.0 - half)) * (2.0 * root + (6.0 * root * 0.044715) * v2)
            hidden_round = (act_grad * slope).astype(BF16)
            big_drop[hs, :] += dot(act.astype(BF16), ct, ((1,), (1,)))
            big_lift[hs, :] += dot(hidden_round, lifted_one, ((1,), (1,)))
            lifted_grad = lifted_grad + dot(lift[:, hs], hidden_round)
        gain_acc[...] += fold(lifted_grad * normed)
        shift_acc[...] += fold(lifted_grad)
        ng = lifted_grad * gain[...]
        m1 = jnp.mean(ng, axis=0, keepdims=True)
        m2 = jnp.mean(ng * normed, axis=0, keepdims=True)
        pg = (inverse * (ng - m1 - normed * m2)).astype(BF16).astype(F32)
        for j in range(step_rows):
            dmain[d.reach + r0 + j] = pg[:, j * d.cols : (j + 1) * d.cols]
        return carry

    lax.fori_loop(0, d.rows // step_rows, step, 0)


def kernel(
    d,
    saved, scale, mask, upstream, taps, offset, gain, shift, lift_t, lift, bias, drop,
    out, big_lift, big_drop, small,
    flat, main, side, dmain, dside, cot, pre, rows_out, rows_in, pack_out, pack_in, fwd_in,
    gain_acc, shift_acc, ssem, rsem,
):
    me, north, south, east, west = neighbours(d)
    peers = [north, south, west] if d.same else [north, south, west, east]
    barrier = pltpu.get_barrier_semaphore()
    for peer in peers:
        pl.semaphore_signal(barrier, inc=1, device_id={"lon": peer}, device_id_type=MESH)
    flat[...] = saved[0].astype(F32).reshape(d.c * d.rows, d.cols)
    for r in range(d.rows):
        row = flat[pl.ds(r, d.c, stride=d.rows), :]
        main[d.reach + r] = (row * scale[...]).astype(BF16).astype(F32)
    pl.semaphore_wait(barrier, len(peers))

    def ex(i, m, s):
        return exchange(
            d, m, s, rows_out.at[i], rows_in.at[i], pack_out.at[i], pack_in.at[i], fwd_in.at[i],
            ssem.at[i], rsem.at[i],
        )

    finish = ex(0, main, side)
    flat[...] = upstream[0].astype(F32).reshape(d.c * d.rows, d.cols)
    for r in range(d.rows):
        row = flat[pl.ds(r, d.c, stride=d.rows), :]
        cot[r] = (row * mask[...]).astype(BF16)
    finish()

    def start(g, at):
        return jnp.broadcast_to(offset[at, :][None], (d.rows, 8, d.cols))

    def store(g, at, acc):
        pre[:, at, :] = acc

    depthwise(d, main, side, taps, False, start, store)
    mlp(d, pre, cot, gain, shift, lift_t, lift, bias, drop, dmain, big_lift, big_drop, gain_acc, shift_acc)
    finish = ex(1, dmain, dside)
    taps_n = d.span * d.span
    lane = lanes((d.c, d.cols))
    small[...] = jnp.where(
        lane == taps_n + 1,
        jnp.sum(gain_acc[...], axis=1, keepdims=True),
        jnp.where(lane == taps_n + 2, jnp.sum(shift_acc[...], axis=1, keepdims=True), 0.0),
    )
    kernel_grads(d, main, side, dmain, small)
    finish()

    def start_back(g, at):
        return jnp.zeros((d.rows, 8, d.cols), F32)

    depthwise(d, dmain, dside, taps, True, start_back, store)
    for r in range(d.rows):
        flat[pl.ds(r, d.c, stride=d.rows), :] = mask[...] * (pre[r] + cot[r].astype(F32))
    out[0] = flat[...].reshape(d.c, d.rows, d.cols).astype(BF16)


def body(
    n,
    saved_input,
    tile_scale,
    ocean_tiles,
    upstream,
    kernel_taps,
    kernel_offset,
    norm_gain,
    norm_shift,
    lift_weight,
    lift_bias,
    drop_weight,
):
    channels, rows, cols = saved_input.shape[1:]
    hidden = lift_weight.shape[1]
    taps_n = kernel_taps.shape[0]
    d = Dims(n, channels, rows, cols, math.isqrt(taps_n), hidden)
    mask = jnp.repeat(ocean_tiles[0], rows).astype(F32)[None]
    scale = jnp.repeat(tile_scale[0].T, rows, axis=1) * mask
    taps = jnp.pad(kernel_taps.T, ((0, 0), (0, 128 - taps_n)))
    vmem = pl.BlockSpec(memory_space=pltpu.VMEM)
    grid3 = (d.ext, channels, cols)
    out, big_lift, big_drop, small = pl.pallas_call(
        functools.partial(kernel, d),
        out_shape=(
            jax.ShapeDtypeStruct((1, channels, rows, cols), BF16),
            jax.ShapeDtypeStruct((hidden, channels + 64), F32),
            jax.ShapeDtypeStruct((hidden, channels), F32),
            jax.ShapeDtypeStruct((channels, cols), F32),
        ),
        in_specs=[vmem] * 12,
        out_specs=(vmem,) * 4,
        scratch_shapes=[
            pltpu.VMEM((channels * rows, cols), F32),
            pltpu.VMEM(grid3, F32),
            pltpu.VMEM(grid3, F32),
            pltpu.VMEM(grid3, F32),
            pltpu.VMEM(grid3, F32),
            pltpu.VMEM((rows, channels, cols), BF16),
            pltpu.VMEM((rows, channels, cols), F32),
            pltpu.VMEM((2, 2, d.reach, channels, cols), BF16),
            pltpu.VMEM((2, 2, d.reach, channels, cols), BF16),
            pltpu.VMEM((2, channels, cols), BF16),
            pltpu.VMEM((2, 2, channels, cols), BF16),
            pltpu.VMEM((2, 2, 2, channels, cols), BF16),
            pltpu.VMEM((channels, cols), F32),
            pltpu.VMEM((channels, cols), F32),
            pltpu.SemaphoreType.DMA((2, 8)),
            pltpu.SemaphoreType.DMA((2, 8)),
        ],
        compiler_params=pltpu.CompilerParams(
            collective_id=0, has_side_effects=True, vmem_limit_bytes=56 * 1024 * 1024
        ),
        name="block_backward",
    )(
        saved_input,
        scale,
        mask,
        upstream,
        taps,
        kernel_offset[:, None],
        norm_gain[:, None],
        norm_shift[:, None],
        lift_weight.T,
        lift_weight,
        lift_bias[:, None],
        drop_weight,
    )
    big_lift, big_drop, small = lax.psum((big_lift, big_drop, small), "lon")
    factor = 1.0 / math.sqrt(n * rows * cols)
    small_t = small.T * factor
    return (
        out,
        small_t[:taps_n],
        small_t[taps_n],
        small_t[taps_n + 1],
        small_t[taps_n + 2],
        big_lift[:, :channels].T * factor,
        big_lift[:, channels] * factor,
        big_drop * factor,
    )


def solution(mesh):
    return jax.shard_map(
        functools.partial(body, mesh.shape["lon"]),
        mesh=mesh,
        in_specs=(
            P(("ens", "lon"), None, None, None),
            P(("ens", "lon"), None, None),
            P(("ens", "lon"), None),
            P(("ens", "lon"), None, None, None),
            P(),
            P(),
            P(),
            P(),
            P(),
            P(),
            P(),
        ),
        out_specs=(
            P(("ens", "lon"), None, None, None),
            P("ens", None),
            P("ens"),
            P("ens"),
            P("ens"),
            P("ens", None),
            P("ens"),
            P("ens", None),
        ),
        check_vma=False,
    )
```

```python
import functools
import math

import jax
import jax.numpy as jnp
from jax import lax
from jax.experimental import pallas as pl
from jax.experimental.pallas import tpu as pltpu
from jax.sharding import PartitionSpec as P

LAT_DEVS = 8
EPSILON = 1e-06
MESH = pl.DeviceIdType.MESH
F32 = jnp.float32
BF16 = jnp.bfloat16


def lanes(shape):
    return lax.broadcasted_iota(jnp.int32, shape, len(shape) - 1)


def roll(x, shift):
    shift = shift % x.shape[-1]
    return x if shift == 0 else pltpu.roll(x, shift, x.ndim - 1)


class Dims:
    def __init__(self, n, channels, rows, cols, span, hidden):
        self.n, self.c, self.rows, self.cols, self.hidden = n, channels, rows, cols, hidden
        self.span, self.reach = span, span // 2
        self.ext = rows + 2 * self.reach
        self.same = 2 * LAT_DEVS == n
        self.group = 2 * LAT_DEVS


def neighbours(d):
    me = lax.axis_index("lon")
    north = lax.rem(me + d.n - 1, d.n)
    south = lax.rem(me + 1, d.n)
    east = lax.rem(me + LAT_DEVS, d.n)
    west = lax.rem(me + d.n - LAT_DEVS, d.n)
    return me, north, south, east, west


def pack_sides(d, main):
    k, r3 = d.reach, d.rows * d.reach

    def step(g, _):
        at = pl.ds(pl.multiple_of(g * 16, 16), 16)
        lane = lanes((16, d.cols))
        packed = jnp.zeros((16, d.cols), F32)
        for r in range(d.rows):
            x = main[r + k, at, :]
            lo, hi = r * k, r3 + r * k
            packed = jnp.where((lane >= lo) & (lane < lo + k), roll(x, lo), packed)
            packed = jnp.where((lane >= hi) & (lane < hi + k), roll(x, hi - (d.cols - k)), packed)
        return at, packed

    return step


def exchange(d, main, side, rows_out, rows_in, pack_out, pack_in, fwd_in, ssem, rsem):
    k = d.reach
    me, north, south, east, west = neighbours(d)

    def copy(src, dst, slot, peer):
        return pltpu.make_async_remote_copy(
            src_ref=src,
            dst_ref=dst,
            send_sem=ssem.at[slot],
            recv_sem=rsem.at[slot],
            device_id={"lon": peer},
            device_id_type=MESH,
        )

    for r in range(k):
        rows_out[0, r] = main[k + r].astype(BF16)
        rows_out[1, r] = main[d.rows + r].astype(BF16)
    to_north = copy(rows_out.at[0], rows_in.at[1], 0, north)
    to_south = copy(rows_out.at[1], rows_in.at[0], 1, south)
    to_north.start()
    to_south.start()
    build = pack_sides(d, main)

    def pack_step(g, carry):
        at, packed = build(g, None)
        pack_out[at, :] = packed.astype(BF16)
        return carry

    lax.fori_loop(0, d.c // 16, pack_step, 0)
    count = 1 if d.same else 2
    sides = [copy(pack_out, pack_in.at[0], 2, west)]
    if not d.same:
        sides.append(copy(pack_out, pack_in.at[1], 3, east))
    for one in sides:
        one.start()

    def finish():
        for one in sides:
            one.wait()
        forwards = []
        for j in range(count):
            forwards.append(copy(pack_in.at[j], fwd_in.at[0, j], 4 + j, south))
            forwards.append(copy(pack_in.at[j], fwd_in.at[1, j], 6 + j, north))
        for one in forwards:
            one.start()
        place = lax.rem(me + 1, LAT_DEVS)
        keep_lower = jnp.where(place != 0, 1.0, 0.0).astype(F32)
        keep_upper = jnp.where(place != LAT_DEVS - 1, 1.0, 0.0).astype(F32)
        r3 = d.rows * k
        last = count - 1

        def unpack(east_pack, west_pack, r):
            lane = lanes(east_pack.shape)
            right = roll(east_pack, -(r * k))
            left = roll(west_pack, (d.cols - k) - (r3 + r * k))
            return jnp.where(lane < d.cols // 2, right, left)

        def own_step(g, carry):
            at = pl.ds(pl.multiple_of(g * 16, 16), 16)
            e, w = pack_in[0, at, :].astype(F32), pack_in[last, at, :].astype(F32)
            for r in range(d.rows):
                side[k + r, at, :] = unpack(e, w, r)
            return carry

        lax.fori_loop(0, d.c // 16, own_step, 0)
        to_north.wait()
        to_south.wait()
        for r in range(k):
            main[r] = rows_in[0, r].astype(F32) * keep_lower
            main[k + d.rows + r] = rows_in[1, r].astype(F32) * keep_upper
        for one in forwards:
            one.wait()

        def corner_step(g, carry):
            at = pl.ds(pl.multiple_of(g * 16, 16), 16)
            ne, nw = fwd_in[0, 0, at, :].astype(F32), fwd_in[0, last, at, :].astype(F32)
            se, sw = fwd_in[1, 0, at, :].astype(F32), fwd_in[1, last, at, :].astype(F32)
            for r in range(k):
                side[r, at, :] = unpack(ne, nw, d.rows - k + r) * keep_lower
                side[k + d.rows + r, at, :] = unpack(se, sw, r) * keep_upper
            return carry

        lax.fori_loop(0, d.c // 16, corner_step, 0)

    return finish


def shifted(d, main, side, at, q):
    s = q - d.reach
    x = main[:, at, :]
    if s == 0:
        return x
    lane = lanes(x.shape)
    h = side[:, at, :]
    keep = lane < s if s > 0 else lane >= d.cols + s
    return roll(jnp.where(keep, h, x), -s)


def depthwise(d, main, side, taps, flip, start, store, first, last):
    def group(g, carry):
        at = pl.ds(pl.multiple_of(g * 8, 8), 8)
        weights = taps[at, :]
        acc = start(g, at)
        for q in range(d.span):
            xq = shifted(d, main, side, at, q)
            for p in range(d.span):
                t = p * d.span + q
                if flip:
                    t = d.span * d.span - 1 - t
                acc = acc + weights[:, t : t + 1][None] * xq[p : p + d.rows]
        store(g, at, acc)
        return carry

    lax.fori_loop(first, last, group, 0)


def kernel_grads(d, main, side, dmain, small):
    def group(g, carry):
        at = pl.ds(pl.multiple_of(g * 8, 8), 8)
        grad = dmain[d.reach : d.reach + d.rows, at, :]
        lane = lanes((8, d.cols))
        out = small[at, :]
        total = jnp.sum(jnp.sum(grad, axis=0), axis=1, keepdims=True)
        out = jnp.where(lane == d.span * d.span, total, out)
        for q in range(d.span):
            xq = shifted(d, main, side, at, q)
            for p in range(d.span):
                term = jnp.sum(grad * xq[p : p + d.rows], axis=0)
                total = jnp.sum(term, axis=1, keepdims=True)
                out = jnp.where(lane == p * d.span + q, total, out)
        small[at, :] = out
        return carry

    lax.fori_loop(0, d.c // 8, group, 0)


def dot(a, b, dims=((1,), (0,))):
    return lax.dot_general(a, b, (dims, ((), ())), preferred_element_type=F32)


def mlp(d, pre, cot, columns, lift_t, lift, drop, dmain, big_lift, big_drop, gain_acc, shift_acc):
    step_rows = 4
    block = 256
    wide = step_rows * d.cols
    root = math.sqrt(2.0 / math.pi)
    big_lift[...] = jnp.zeros_like(big_lift)
    big_drop[...] = jnp.zeros_like(big_drop)
    gain_acc[...] = jnp.zeros_like(gain_acc)
    shift_acc[...] = jnp.zeros_like(shift_acc)
    at = d.span * d.span
    gain = columns[: d.c, at + 1 : at + 2]
    shift = columns[: d.c, at + 2 : at + 3]

    def fold(x):
        return sum(x[:, j * d.cols : (j + 1) * d.cols] for j in range(step_rows))

    def step(i, carry):
        r0 = i * step_rows
        x = jnp.concatenate([pre[r0 + j] for j in range(step_rows)], axis=1)
        ct = jnp.concatenate([cot[r0 + j] for j in range(step_rows)], axis=1)
        centre = x - jnp.mean(x, axis=0, keepdims=True)
        inverse = lax.rsqrt(jnp.mean(centre * centre, axis=0, keepdims=True) + EPSILON)
        normed = centre * inverse
        lifted = (normed * gain + shift).astype(BF16)
        ones = jnp.where(
            lax.broadcasted_iota(jnp.int32, (64, wide), 0) == 0, 1.0, 0.0
        ).astype(BF16)
        lifted_one = jnp.concatenate([lifted, ones], axis=0)
        gap = jnp.zeros((64, wide), BF16)
        ct_apart = jnp.concatenate([ct[:128], gap, ct[128:]], axis=0)
        lifted_grad = jnp.zeros((d.c, wide), F32)
        for b in range(d.hidden // block):
            hs = slice(b * block, (b + 1) * block)
            v = dot(lift_t[hs, :], lifted) + columns[:, at + 3 + b : at + 4 + b]
            act_grad = dot(drop[hs, :], ct)
            v2 = v * v
            half = 0.5 * jnp.tanh(v * (root + (root * 0.044715) * v2)) + 0.5
            act = v * half
            slope = half + (act * (1.0 - half)) * (2.0 * root + (6.0 * root * 0.044715) * v2)
            hidden_round = (act_grad * slope).astype(BF16)
            big_drop[hs, :] += dot(act.astype(BF16), ct_apart, ((1,), (1,)))
            big_lift[hs, :] += dot(hidden_round, lifted_one, ((1,), (1,)))
            lifted_grad = lifted_grad + dot(lift[:, hs], hidden_round)
        gain_acc[...] += fold(lifted_grad * normed)
        shift_acc[...] += fold(lifted_grad)
        ng = lifted_grad * gain
        m1 = jnp.mean(ng, axis=0, keepdims=True)
        m2 = jnp.mean(ng * normed, axis=0, keepdims=True)
        pg = (inverse * (ng - m1 - normed * m2)).astype(BF16).astype(F32)
        for j in range(step_rows):
            dmain[d.reach + r0 + j] = pg[:, j * d.cols : (j + 1) * d.cols]
        return carry

    lax.fori_loop(0, d.rows // step_rows, step, 0)


def remote(src, dst, ssem, rsem, peer):
    return pltpu.make_async_remote_copy(
        src_ref=src,
        dst_ref=dst,
        send_sem=ssem,
        recv_sem=rsem,
        device_id={"lon": peer},
        device_id_type=MESH,
    )


class Sums:
    def __init__(self, d, bufs, factor):
        self.d, self.factor = d, factor
        (self.mine, self.from_core, self.pair, self.from_chip, self.all, self.small, self.small_in,
         self.small_all, self.csem, self.hsem, self.gsem, self.dsem, self.rsem, self.asem) = bufs
        me = lax.axis_index("lon")
        self.chips = d.group // 2
        self.rank = lax.rem(me, d.group)
        self.base = me - self.rank
        self.core = lax.rem(self.rank, 2)
        self.chip = self.rank // 2
        self.partner = self.base + self.chip * 2 + (1 - self.core)

    def chip_peer(self, t):
        other = lax.rem(self.chip + t, self.chips)
        return other, self.base + other * 2 + self.core

    def start_pair(self, big_lift, big_drop):
        chunk = self.mine.shape[2]
        lane = lanes((chunk, 128))
        for h in range(2):
            for c in range(self.chips):
                at = slice((h * self.chips + c) * chunk, (h * self.chips + c + 1) * chunk)
                middle = jnp.where(lane < 64, big_lift[at, 128:], big_drop[at, 128:])
                self.mine[h, c, :, 0:128] = big_lift[at, :128].astype(BF16)
                self.mine[h, c, :, 128:256] = middle.astype(BF16)
                self.mine[h, c, :, 256:384] = big_drop[at, :128].astype(BF16)
        self.pair_copy = remote(
            self.mine.at[1 - self.core], self.from_core, self.csem.at[0], self.csem.at[1], self.partner
        )
        self.pair_copy.start()

    def start_chips(self):
        self.pair_copy.wait()
        for c in range(self.chips):
            self.pair[c] = (self.mine[self.core, c].astype(F32) + self.from_core[c].astype(F32)).astype(BF16)
        self.chip_copies = []
        for t in range(1, self.chips):
            other, peer = self.chip_peer(t)
            self.chip_copies.append(
                remote(self.pair.at[other], self.from_chip.at[t - 1], self.hsem.at[0, t], self.hsem.at[1, t], peer)
            )
        for one in self.chip_copies:
            one.start()

    def start_gather(self):
        for one in self.chip_copies:
            one.wait()
        total = self.pair[self.chip].astype(F32)
        for t in range(1, self.chips):
            total = total + self.from_chip[t - 1].astype(F32)
        self.all[self.core, self.chip] = (total * self.factor).astype(BF16)
        self.gathers = []
        for t in range(1, self.chips):
            other, peer = self.chip_peer(t)
            place = self.all.at[self.core, self.chip]
            self.gathers.append(remote(place, place, self.gsem.at[0, t], self.gsem.at[1, t], peer))
        for one in self.gathers:
            one.start()

    def start_back(self):
        for one in self.gathers:
            one.wait()
        half = self.all.at[self.core]
        self.back = remote(half, half, self.dsem.at[0], self.dsem.at[1], self.partner)
        self.back.start()

    def finish(self, out_lift, out_drop):
        self.back.wait()
        rows = self.chips * self.mine.shape[2]
        for h in range(2):
            at = slice(h * rows, (h + 1) * rows)
            part = self.all[h].reshape(rows, 384).astype(F32)
            middle = part[:, 128:256]
            out_drop[at, 0:128] = part[:, 256:]
            out_drop[at, 128:192] = roll(middle, 64)[:, :64]
            out_lift[0:128, at] = part[:, :128].T
            out_lift[128:192, at] = middle.T[:64]

    def start_small(self):
        self.small_copies = []
        for t in range(1, self.d.group):
            other = lax.rem(self.rank + t, self.d.group)
            self.small_copies.append(
                remote(self.small.at[other], self.small_in.at[t - 1], self.rsem.at[0, t], self.rsem.at[1, t], self.base + other)
            )
        for one in self.small_copies:
            one.start()

    def start_small_gather(self):
        for one in self.small_copies:
            one.wait()
        total = self.small[self.rank]
        for t in range(1, self.d.group):
            total = total + self.small_in[t - 1]
        self.small_all[self.rank] = total * self.factor
        self.small_copies = []
        for t in range(1, self.d.group):
            other = lax.rem(self.rank + t, self.d.group)
            place = self.small_all.at[self.rank]
            self.small_copies.append(
                remote(place, place, self.asem.at[0, t], self.asem.at[1, t], self.base + other)
            )
        for one in self.small_copies:
            one.start()

    def finish_small(self):
        for one in self.small_copies:
            one.wait()
        return self.small_all[...].reshape(128, 128)


def kernel(
    d, factor,
    saved, tile_scale, ocean, upstream, taps, offset, gain, shift, lift, bias, drop,
    out, out_taps, out_offset, out_gain, out_shift, out_lift, out_bias, out_drop,
    flat, main, side, dmain, dside, cot, pre, rows_out, rows_in, pack_out, pack_in, fwd_in,
    gain_acc, shift_acc, ssem, rsem, columns, lift_t, big_lift, big_drop, small_cols, *bufs,
):
    me, north, south, east, west = neighbours(d)
    sums = Sums(d, bufs, factor)
    peers = [sums.base + lax.rem(sums.rank + t, d.group) for t in range(1, d.group)]
    if d.n != d.group:
        peers += [north, south, east, west]
    barrier = pltpu.get_barrier_semaphore()
    for peer in peers:
        pl.semaphore_signal(barrier, inc=1, device_id={"lon": peer}, device_id_type=MESH)
    taps_n = d.span * d.span
    wide = 256
    blocks = d.hidden // wide
    slots = tile_scale.shape[1]
    pad = jnp.zeros((1, wide - d.c), F32)

    def widen(x):
        return jnp.concatenate([x, jnp.broadcast_to(pad, (x.shape[0], wide - d.c))], axis=1)

    rows = flat.at[0:256]
    rows[...] = jnp.zeros_like(rows)
    for h, (lo, hi) in enumerate(((0, 128), (128, d.c))):
        at = slice(h * 128, h * 128 + taps_n)
        rows[at, 0 : hi - lo] = taps[:, lo:hi]
        for k, one in enumerate((offset, gain, shift)):
            rows[h * 128 + taps_n + k : h * 128 + taps_n + k + 1, 0 : hi - lo] = one[:, lo:hi]
        for b in range(blocks):
            rows[h * 128 + taps_n + 3 + b : h * 128 + taps_n + 4 + b, :] = bias[
                :, b * wide + h * 128 : b * wide + h * 128 + 128
            ]
        rows[h * 128 + 56 : h * 128 + 56 + slots, 0 : hi - lo] = tile_scale[0, :, lo:hi]
        columns[h * 128 : h * 128 + 128, :] = rows[h * 128 : h * 128 + 128, :].T
    lane = lanes((1, d.cols))
    mask = jnp.zeros((1, d.cols), F32)
    scale = jnp.zeros((d.c, d.cols), F32)
    for s in range(slots):
        here = (lane >= s * d.rows) & (lane < (s + 1) * d.rows)
        mask = jnp.where(here, ocean[:, s : s + 1].astype(F32), mask)
        scale = jnp.where(here, columns[: d.c, 56 + s : 57 + s], scale)
    scale = scale * mask
    lift_t[...] = lift[...].astype(F32).T.astype(BF16)
    flat[...] = saved[0].astype(F32).reshape(d.c * d.rows, d.cols)
    for r in range(d.rows):
        row = flat[pl.ds(r, d.c, stride=d.rows), :]
        main[d.reach + r] = (row * scale).astype(BF16).astype(F32)
    pl.semaphore_wait(barrier, len(peers))

    def ex(i, m, s):
        return exchange(
            d, m, s, rows_out.at[i], rows_in.at[i], pack_out.at[i], pack_in.at[i], fwd_in.at[i],
            ssem.at[i], rsem.at[i],
        )

    finish = ex(0, main, side)
    flat[...] = upstream[0].astype(F32).reshape(d.c * d.rows, d.cols)
    for r in range(d.rows):
        row = flat[pl.ds(r, d.c, stride=d.rows), :]
        cot[r] = (row * mask).astype(BF16)
    finish()

    def start(g, at):
        return jnp.broadcast_to(columns[at, taps_n : taps_n + 1][None], (d.rows, 8, d.cols))

    def store(g, at, acc):
        pre[:, at, :] = acc

    groups = d.c // 8
    depthwise(d, main, side, columns, False, start, store, 0, groups)
    mlp(d, pre, cot, columns, lift_t, lift, drop, dmain, big_lift, big_drop, gain_acc, shift_acc)
    finish = ex(1, dmain, dside)
    sums.start_pair(big_lift, big_drop)
    lane = lanes((d.c, d.cols))
    small_cols[...] = jnp.zeros_like(small_cols)
    small_cols[: d.c, :] = jnp.where(
        lane == taps_n + 1,
        jnp.sum(gain_acc[...], axis=1, keepdims=True),
        jnp.where(lane == taps_n + 2, jnp.sum(shift_acc[...], axis=1, keepdims=True), 0.0),
    )
    kernel_grads(d, main, side, dmain, small_cols)
    lane = lanes((wide, d.cols))
    for b in range(blocks):
        column = big_lift[b * wide : (b + 1) * wide, d.c : d.c + 1]
        small_cols[...] = jnp.where(lane == taps_n + 3 + b, column, small_cols[...])
    for h in range(2):
        turned = small_cols[h * 128 : h * 128 + 128, :].T
        for i in range(8):
            sums.small[h * 8 + i] = turned[i * 8 : i * 8 + 8]
    sums.start_chips()
    sums.start_small()
    finish()

    def start_back(g, at):
        return jnp.zeros((d.rows, 8, d.cols), F32)

    third = groups // 3
    depthwise(d, dmain, dside, columns, True, start_back, store, 0, third)
    sums.start_gather()
    sums.start_small_gather()
    depthwise(d, dmain, dside, columns, True, start_back, store, third, 2 * third)
    sums.start_back()
    depthwise(d, dmain, dside, columns, True, start_back, store, 2 * third, groups)
    for r in range(d.rows):
        flat[pl.ds(r, d.c, stride=d.rows), :] = mask * (pre[r] + cot[r].astype(F32))
    out[0] = flat[...].reshape(d.c, d.rows, d.cols).astype(BF16)
    small = sums.finish_small()
    for h, (lo, hi) in enumerate(((0, 128), (128, d.c))):
        base = h * 64
        out_taps[:, lo:hi] = small[base : base + taps_n, 0 : hi - lo]
        for k, one in enumerate((out_offset, out_gain, out_shift)):
            one[:, lo:hi] = small[base + taps_n + k : base + taps_n + k + 1, 0 : hi - lo]
        for b in range(blocks):
            out_bias[:, b * wide + h * 128 : b * wide + h * 128 + 128] = small[
                base + taps_n + 3 + b : base + taps_n + 4 + b
            ]
    sums.finish(out_lift, out_drop)


def body(
    n,
    saved_input,
    tile_scale,
    ocean_tiles,
    upstream,
    kernel_taps,
    kernel_offset,
    norm_gain,
    norm_shift,
    lift_weight,
    lift_bias,
    drop_weight,
):
    channels, rows, cols = saved_input.shape[1:]
    hidden = lift_weight.shape[1]
    taps_n = kernel_taps.shape[0]
    d = Dims(n, channels, rows, cols, math.isqrt(taps_n), hidden)
    vmem = pl.BlockSpec(memory_space=pltpu.VMEM)
    grid3 = (d.ext, channels, cols)
    factor = 1.0 / math.sqrt(n * rows * cols)
    chips = d.group // 2
    chunk = hidden // d.group
    dma = pltpu.SemaphoreType.DMA
    out, *grads = pl.pallas_call(
        functools.partial(kernel, d, factor),
        out_shape=(
            jax.ShapeDtypeStruct((1, channels, rows, cols), BF16),
            jax.ShapeDtypeStruct((taps_n, channels), F32),
            jax.ShapeDtypeStruct((1, channels), F32),
            jax.ShapeDtypeStruct((1, channels), F32),
            jax.ShapeDtypeStruct((1, channels), F32),
            jax.ShapeDtypeStruct((channels, hidden), F32),
            jax.ShapeDtypeStruct((1, hidden), F32),
            jax.ShapeDtypeStruct((hidden, channels), F32),
        ),
        in_specs=[vmem] * 11,
        out_specs=(vmem,) * 8,
        scratch_shapes=[
            pltpu.VMEM((channels * rows, cols), F32),
            pltpu.VMEM(grid3, F32),
            pltpu.VMEM(grid3, F32),
            pltpu.VMEM(grid3, F32),
            pltpu.VMEM(grid3, F32),
            pltpu.VMEM((rows, channels, cols), BF16),
            pltpu.VMEM((rows, channels, cols), F32),
            pltpu.VMEM((2, 2, d.reach, channels, cols), BF16),
            pltpu.VMEM((2, 2, d.reach, channels, cols), BF16),
            pltpu.VMEM((2, channels, cols), BF16),
            pltpu.VMEM((2, 2, channels, cols), BF16),
            pltpu.VMEM((2, 2, 2, channels, cols), BF16),
            pltpu.VMEM((channels, cols), F32),
            pltpu.VMEM((channels, cols), F32),
            dma((2, 8)),
            dma((2, 8)),
            pltpu.VMEM((256, 128), F32),
            pltpu.VMEM((hidden, channels), BF16),
            pltpu.VMEM((hidden, 256), F32),
            pltpu.VMEM((hidden, 256), F32),
            pltpu.VMEM((256, 128), F32),
            pltpu.VMEM((2, chips, chunk, 384), BF16),
            pltpu.VMEM((chips, chunk, 384), BF16),
            pltpu.VMEM((chips, chunk, 384), BF16),
            pltpu.VMEM((chips - 1, chunk, 384), BF16),
            pltpu.VMEM((2, chips, chunk, 384), BF16),
            pltpu.VMEM((d.group, 8, 128), F32),
            pltpu.VMEM((d.group - 1, 8, 128), F32),
            pltpu.VMEM((d.group, 8, 128), F32),
            dma((2,)),
            dma((2, chips)),
            dma((2, chips)),
            dma((2,)),
            dma((2, d.group)),
            dma((2, d.group)),
        ],
        compiler_params=pltpu.CompilerParams(
            collective_id=0, has_side_effects=True, vmem_limit_bytes=56 * 1024 * 1024
        ),
        name="block_backward",
    )(
        saved_input,
        tile_scale,
        ocean_tiles,
        upstream,
        kernel_taps,
        kernel_offset[None],
        norm_gain[None],
        norm_shift[None],
        lift_weight,
        lift_bias[None],
        drop_weight,
    )
    if n != d.group:
        across = [[i + d.group * k for k in range(n // d.group)] for i in range(d.group)]
        grads = lax.psum(grads, "lon", axis_index_groups=across)
    g_taps, g_offset, g_gain, g_shift, g_lift, g_bias, g_drop = grads
    return (out, g_taps, g_offset[0], g_gain[0], g_shift[0], g_lift, g_bias[0], g_drop)


def solution(mesh):
    return jax.shard_map(
        functools.partial(body, mesh.shape["lon"]),
        mesh=mesh,
        in_specs=(
            P(("ens", "lon"), None, None, None),
            P(("ens", "lon"), None, None),
            P(("ens", "lon"), None),
            P(("ens", "lon"), None, None, None),
            P(),
            P(),
            P(),
            P(),
            P(),
            P(),
            P(),
        ),
        out_specs=(
            P(("ens", "lon"), None, None, None),
            P("ens", None),
            P("ens"),
            P("ens"),
            P("ens"),
            P("ens", None),
            P("ens"),
            P("ens", None),
        ),
        check_vma=False,
    )
```

```python
import functools
import math

import jax
import jax.numpy as jnp
from jax import lax
from jax.experimental import pallas as pl
from jax.experimental.pallas import tpu as pltpu
from jax.sharding import PartitionSpec as P

LAT_DEVS = 8
EPSILON = 1e-06
MESH = pl.DeviceIdType.MESH
F32 = jnp.float32
BF16 = jnp.bfloat16


def lanes(shape):
    return lax.broadcasted_iota(jnp.int32, shape, len(shape) - 1)


def roll(x, shift):
    shift = shift % x.shape[-1]
    return x if shift == 0 else pltpu.roll(x, shift, x.ndim - 1)


class Dims:
    def __init__(self, n, channels, rows, cols, span, hidden):
        self.n, self.c, self.rows, self.cols, self.hidden = n, channels, rows, cols, hidden
        self.span, self.reach = span, span // 2
        self.ext = rows + 2 * self.reach
        self.same = 2 * LAT_DEVS == n
        self.group = 2 * LAT_DEVS


def neighbours(d):
    me = lax.axis_index("lon")
    north = lax.rem(me + d.n - 1, d.n)
    south = lax.rem(me + 1, d.n)
    east = lax.rem(me + LAT_DEVS, d.n)
    west = lax.rem(me + d.n - LAT_DEVS, d.n)
    return me, north, south, east, west


def pack_sides(d, main):
    k, r3 = d.reach, d.rows * d.reach

    def step(g, _):
        at = pl.ds(pl.multiple_of(g * 16, 16), 16)
        lane = lanes((16, d.cols))
        packed = jnp.zeros((16, d.cols), F32)
        for r in range(d.rows):
            x = main[r + k, at, :]
            lo, hi = r * k, r3 + r * k
            packed = jnp.where((lane >= lo) & (lane < lo + k), roll(x, lo), packed)
            packed = jnp.where((lane >= hi) & (lane < hi + k), roll(x, hi - (d.cols - k)), packed)
        return at, packed

    return step


def exchange(d, main, side, rows_out, rows_in, pack_out, pack_in, fwd_in, ssem, rsem):
    k = d.reach
    me, north, south, east, west = neighbours(d)

    def copy(src, dst, slot, peer):
        return pltpu.make_async_remote_copy(
            src_ref=src,
            dst_ref=dst,
            send_sem=ssem.at[slot],
            recv_sem=rsem.at[slot],
            device_id={"lon": peer},
            device_id_type=MESH,
        )

    for r in range(k):
        rows_out[0, r] = main[k + r].astype(BF16)
        rows_out[1, r] = main[d.rows + r].astype(BF16)
    to_north = copy(rows_out.at[0], rows_in.at[1], 0, north)
    to_south = copy(rows_out.at[1], rows_in.at[0], 1, south)
    to_north.start()
    to_south.start()
    build = pack_sides(d, main)

    def pack_step(g, carry):
        at, packed = build(g, None)
        pack_out[at, :] = packed.astype(BF16)
        return carry

    lax.fori_loop(0, d.c // 16, pack_step, 0)
    count = 1 if d.same else 2
    sides = [copy(pack_out, pack_in.at[0], 2, west)]
    if not d.same:
        sides.append(copy(pack_out, pack_in.at[1], 3, east))
    for one in sides:
        one.start()

    def finish():
        for one in sides:
            one.wait()
        forwards = []
        for j in range(count):
            forwards.append(copy(pack_in.at[j], fwd_in.at[0, j], 4 + j, south))
            forwards.append(copy(pack_in.at[j], fwd_in.at[1, j], 6 + j, north))
        for one in forwards:
            one.start()
        place = lax.rem(me + 1, LAT_DEVS)
        keep_lower = jnp.where(place != 0, 1.0, 0.0).astype(F32)
        keep_upper = jnp.where(place != LAT_DEVS - 1, 1.0, 0.0).astype(F32)
        r3 = d.rows * k
        last = count - 1

        def unpack(east_pack, west_pack, r):
            lane = lanes(east_pack.shape)
            right = roll(east_pack, -(r * k))
            left = roll(west_pack, (d.cols - k) - (r3 + r * k))
            return jnp.where(lane < d.cols // 2, right, left)

        def own_step(g, carry):
            at = pl.ds(pl.multiple_of(g * 16, 16), 16)
            e, w = pack_in[0, at, :].astype(F32), pack_in[last, at, :].astype(F32)
            for r in range(d.rows):
                side[k + r, at, :] = unpack(e, w, r)
            return carry

        lax.fori_loop(0, d.c // 16, own_step, 0)
        to_north.wait()
        to_south.wait()
        for r in range(k):
            main[r] = rows_in[0, r].astype(F32) * keep_lower
            main[k + d.rows + r] = rows_in[1, r].astype(F32) * keep_upper
        for one in forwards:
            one.wait()

        def corner_step(g, carry):
            at = pl.ds(pl.multiple_of(g * 16, 16), 16)
            ne, nw = fwd_in[0, 0, at, :].astype(F32), fwd_in[0, last, at, :].astype(F32)
            se, sw = fwd_in[1, 0, at, :].astype(F32), fwd_in[1, last, at, :].astype(F32)
            for r in range(k):
                side[r, at, :] = unpack(ne, nw, d.rows - k + r) * keep_lower
                side[k + d.rows + r, at, :] = unpack(se, sw, r) * keep_upper
            return carry

        lax.fori_loop(0, d.c // 16, corner_step, 0)

    return finish


def shifted(d, main, side, at, q):
    s = q - d.reach
    x = main[:, at, :]
    if s == 0:
        return x
    lane = lanes(x.shape)
    h = side[:, at, :]
    keep = lane < s if s > 0 else lane >= d.cols + s
    return roll(jnp.where(keep, h, x), -s)


def depthwise(d, main, side, taps, flip, start, store, first, last):
    def group(g, carry):
        at = pl.ds(pl.multiple_of(g * 8, 8), 8)
        weights = taps[at, :]
        acc = start(g, at)
        for q in range(d.span):
            xq = shifted(d, main, side, at, q)
            for p in range(d.span):
                t = p * d.span + q
                if flip:
                    t = d.span * d.span - 1 - t
                acc = acc + weights[:, t : t + 1][None] * xq[p : p + d.rows]
        store(g, at, acc)
        return carry

    lax.fori_loop(first, last, group, 0)


def kernel_grads(d, main, side, dmain, small):
    def group(g, carry):
        at = pl.ds(pl.multiple_of(g * 8, 8), 8)
        grad = dmain[d.reach : d.reach + d.rows, at, :]
        lane = lanes((8, d.cols))
        out = small[at, :]
        total = jnp.sum(jnp.sum(grad, axis=0), axis=1, keepdims=True)
        out = jnp.where(lane == d.span * d.span, total, out)
        for q in range(d.span):
            xq = shifted(d, main, side, at, q)
            for p in range(d.span):
                term = jnp.sum(grad * xq[p : p + d.rows], axis=0)
                total = jnp.sum(term, axis=1, keepdims=True)
                out = jnp.where(lane == p * d.span + q, total, out)
        small[at, :] = out
        return carry

    lax.fori_loop(0, d.c // 8, group, 0)


def dot(a, b, dims=((1,), (0,))):
    return lax.dot_general(a, b, (dims, ((), ())), preferred_element_type=F32)


def mlp(d, pre, cot, columns, lift_t, lift, drop, dmain, big_lift, big_drop, gain_acc, shift_acc):
    step_rows = 4
    block = 256
    wide = step_rows * d.cols
    root = math.sqrt(2.0 / math.pi)
    big_lift[...] = jnp.zeros_like(big_lift)
    big_drop[...] = jnp.zeros_like(big_drop)
    gain_acc[...] = jnp.zeros_like(gain_acc)
    shift_acc[...] = jnp.zeros_like(shift_acc)
    at = d.span * d.span
    gain = columns[: d.c, at + 1 : at + 2]
    shift = columns[: d.c, at + 2 : at + 3]

    def fold(x):
        return sum(x[:, j * d.cols : (j + 1) * d.cols] for j in range(step_rows))

    def step(i, carry):
        r0 = i * step_rows
        x = jnp.concatenate([pre[r0 + j] for j in range(step_rows)], axis=1)
        ct = jnp.concatenate([cot[r0 + j] for j in range(step_rows)], axis=1)
        centre = x - jnp.mean(x, axis=0, keepdims=True)
        inverse = lax.rsqrt(jnp.mean(centre * centre, axis=0, keepdims=True) + EPSILON)
        normed = centre * inverse
        lifted = (normed * gain + shift).astype(BF16)
        ones = jnp.where(
            lax.broadcasted_iota(jnp.int32, (64, wide), 0) == 0, 1.0, 0.0
        ).astype(BF16)
        lifted_one = jnp.concatenate([lifted, ones], axis=0)
        gap = jnp.zeros((64, wide), BF16)
        ct_apart = jnp.concatenate([ct[:128], gap, ct[128:]], axis=0)
        lifted_grad = jnp.zeros((d.c, wide), F32)
        for b in range(d.hidden // block):
            hs = slice(b * block, (b + 1) * block)
            v = dot(lift_t[hs, :], lifted) + columns[:, at + 3 + b : at + 4 + b]
            act_grad = dot(drop[hs, :], ct)
            v2 = v * v
            half = 0.5 * jnp.tanh(v * (root + (root * 0.044715) * v2)) + 0.5
            act = v * half
            slope = half + (act * (1.0 - half)) * (2.0 * root + (6.0 * root * 0.044715) * v2)
            hidden_round = (act_grad * slope).astype(BF16)
            big_drop[hs, :] += dot(act.astype(BF16), ct_apart, ((1,), (1,)))
            big_lift[hs, :] += dot(hidden_round, lifted_one, ((1,), (1,)))
            lifted_grad = lifted_grad + dot(lift[:, hs], hidden_round)
        gain_acc[...] += fold(lifted_grad * normed)
        shift_acc[...] += fold(lifted_grad)
        ng = lifted_grad * gain
        m1 = jnp.mean(ng, axis=0, keepdims=True)
        m2 = jnp.mean(ng * normed, axis=0, keepdims=True)
        pg = (inverse * (ng - m1 - normed * m2)).astype(BF16).astype(F32)
        for j in range(step_rows):
            dmain[d.reach + r0 + j] = pg[:, j * d.cols : (j + 1) * d.cols]
        return carry

    lax.fori_loop(0, d.rows // step_rows, step, 0)


def remote(src, dst, ssem, rsem, peer):
    return pltpu.make_async_remote_copy(
        src_ref=src,
        dst_ref=dst,
        send_sem=ssem,
        recv_sem=rsem,
        device_id={"lon": peer},
        device_id_type=MESH,
    )


class Sums:
    def __init__(self, d, bufs, factor):
        self.d, self.factor = d, factor
        (self.mine, self.from_core, self.pair, self.from_chip, self.all, self.small, self.small_in,
         self.small_all, self.csem, self.hsem, self.gsem, self.dsem, self.rsem, self.asem) = bufs
        me = lax.axis_index("lon")
        self.chips = d.group // 2
        self.rank = lax.rem(me, d.group)
        self.base = me - self.rank
        self.core = lax.rem(self.rank, 2)
        self.chip = self.rank // 2
        self.partner = self.base + self.chip * 2 + (1 - self.core)

    def chip_peer(self, t):
        other = lax.rem(self.chip + t, self.chips)
        return other, self.base + other * 2 + self.core

    def start_pair(self, big_lift, big_drop):
        chunk = self.mine.shape[2]
        lane = lanes((chunk, 128))
        for h in range(2):
            for c in range(self.chips):
                at = slice((h * self.chips + c) * chunk, (h * self.chips + c + 1) * chunk)
                middle = jnp.where(lane < 64, big_lift[at, 128:], big_drop[at, 128:])
                self.mine[h, c, :, 0:128] = big_lift[at, :128].astype(BF16)
                self.mine[h, c, :, 128:256] = middle.astype(BF16)
                self.mine[h, c, :, 256:384] = big_drop[at, :128].astype(BF16)
        self.pair_copy = remote(
            self.mine.at[1 - self.core], self.from_core, self.csem.at[0], self.csem.at[1], self.partner
        )
        self.pair_copy.start()

    def start_chips(self):
        self.pair_copy.wait()
        for c in range(self.chips):
            self.pair[c] = (self.mine[self.core, c].astype(F32) + self.from_core[c].astype(F32)).astype(BF16)
        self.chip_copies = []
        for t in range(1, self.chips):
            other, peer = self.chip_peer(t)
            self.chip_copies.append(
                remote(self.pair.at[other], self.from_chip.at[t - 1], self.hsem.at[0, t], self.hsem.at[1, t], peer)
            )
        for one in self.chip_copies:
            one.start()

    def start_gather(self):
        for one in self.chip_copies:
            one.wait()
        total = self.pair[self.chip].astype(F32)
        for t in range(1, self.chips):
            total = total + self.from_chip[t - 1].astype(F32)
        self.all[self.core, self.chip] = (total * self.factor).astype(BF16)
        self.gathers = []
        for t in range(1, self.chips):
            other, peer = self.chip_peer(t)
            place = self.all.at[self.core, self.chip]
            self.gathers.append(remote(place, place, self.gsem.at[0, t], self.gsem.at[1, t], peer))
        for one in self.gathers:
            one.start()

    def start_back(self):
        for one in self.gathers:
            one.wait()
        half = self.all.at[self.core]
        self.back = remote(half, half, self.dsem.at[0], self.dsem.at[1], self.partner)
        self.back.start()

    def finish(self, out_lift, out_drop):
        self.back.wait()
        rows = self.chips * self.mine.shape[2]
        for h in range(2):
            at = slice(h * rows, (h + 1) * rows)
            part = self.all[h].reshape(rows, 384).astype(F32)
            middle = part[:, 128:256]
            turned = middle.T
            out_drop[0:128, at] = part[:, 256:].T
            out_drop[128:192, at] = turned[64:]
            out_lift[0:128, at] = part[:, :128].T
            out_lift[128:192, at] = turned[:64]

    def start_small(self):
        self.small_copies = []
        for t in range(1, self.d.group):
            other = lax.rem(self.rank + t, self.d.group)
            self.small_copies.append(
                remote(self.small.at[other], self.small_in.at[t - 1], self.rsem.at[0, t], self.rsem.at[1, t], self.base + other)
            )
        for one in self.small_copies:
            one.start()

    def start_small_gather(self):
        for one in self.small_copies:
            one.wait()
        total = self.small[self.rank]
        for t in range(1, self.d.group):
            total = total + self.small_in[t - 1]
        self.small_all[self.rank] = total * self.factor
        self.small_copies = []
        for t in range(1, self.d.group):
            other = lax.rem(self.rank + t, self.d.group)
            place = self.small_all.at[self.rank]
            self.small_copies.append(
                remote(place, place, self.asem.at[0, t], self.asem.at[1, t], self.base + other)
            )
        for one in self.small_copies:
            one.start()

    def finish_small(self):
        for one in self.small_copies:
            one.wait()
        return self.small_all[...].reshape(128, 128)


def kernel(
    d, factor,
    saved, tile_scale, ocean, upstream, taps, offset, gain, shift, lift, bias, drop,
    out, out_taps, out_offset, out_gain, out_shift, out_lift, out_bias, out_drop,
    flat, main, side, dmain, dside, cot, pre, rows_out, rows_in, pack_out, pack_in, fwd_in,
    gain_acc, shift_acc, ssem, rsem, columns, lift_t, drop_t, big_lift, big_drop, small_cols, *bufs,
):
    me, north, south, east, west = neighbours(d)
    sums = Sums(d, bufs, factor)
    peers = [sums.base + lax.rem(sums.rank + t, d.group) for t in range(1, d.group)]
    if d.n != d.group:
        peers += [north, south, east, west]
    barrier = pltpu.get_barrier_semaphore()
    for peer in peers:
        pl.semaphore_signal(barrier, inc=1, device_id={"lon": peer}, device_id_type=MESH)
    taps_n = d.span * d.span
    wide = 256
    blocks = d.hidden // wide
    slots = tile_scale.shape[1]
    pad = jnp.zeros((1, wide - d.c), F32)

    def widen(x):
        return jnp.concatenate([x, jnp.broadcast_to(pad, (x.shape[0], wide - d.c))], axis=1)

    rows = flat.at[0:256]
    rows[...] = jnp.zeros_like(rows)
    for h, (lo, hi) in enumerate(((0, 128), (128, d.c))):
        at = slice(h * 128, h * 128 + taps_n)
        rows[at, 0 : hi - lo] = taps[:, lo:hi]
        for k, one in enumerate((offset, gain, shift)):
            rows[h * 128 + taps_n + k : h * 128 + taps_n + k + 1, 0 : hi - lo] = one[:, lo:hi]
        for b in range(blocks):
            rows[h * 128 + taps_n + 3 + b : h * 128 + taps_n + 4 + b, :] = bias[
                :, b * wide + h * 128 : b * wide + h * 128 + 128
            ]
        rows[h * 128 + 56 : h * 128 + 56 + slots, 0 : hi - lo] = tile_scale[0, :, lo:hi]
        columns[h * 128 : h * 128 + 128, :] = rows[h * 128 : h * 128 + 128, :].T
    lane = lanes((1, d.cols))
    mask = jnp.zeros((1, d.cols), F32)
    scale = jnp.zeros((d.c, d.cols), F32)
    for s in range(slots):
        here = (lane >= s * d.rows) & (lane < (s + 1) * d.rows)
        mask = jnp.where(here, ocean[:, s : s + 1].astype(F32), mask)
        scale = jnp.where(here, columns[: d.c, 56 + s : 57 + s], scale)
    scale = scale * mask
    lift_t[...] = lift[...].astype(F32).T.astype(BF16)
    drop_t[...] = drop[...].astype(F32).T.astype(BF16)
    flat[...] = saved[0].astype(F32).reshape(d.c * d.rows, d.cols)
    for r in range(d.rows):
        row = flat[pl.ds(r, d.c, stride=d.rows), :]
        main[d.reach + r] = (row * scale).astype(BF16).astype(F32)
    pl.semaphore_wait(barrier, len(peers))

    def ex(i, m, s):
        return exchange(
            d, m, s, rows_out.at[i], rows_in.at[i], pack_out.at[i], pack_in.at[i], fwd_in.at[i],
            ssem.at[i], rsem.at[i],
        )

    finish = ex(0, main, side)
    flat[...] = upstream[0].astype(F32).reshape(d.c * d.rows, d.cols)
    for r in range(d.rows):
        row = flat[pl.ds(r, d.c, stride=d.rows), :]
        cot[r] = (row * mask).astype(BF16)
    finish()

    def start(g, at):
        return jnp.broadcast_to(columns[at, taps_n : taps_n + 1][None], (d.rows, 8, d.cols))

    def store(g, at, acc):
        pre[:, at, :] = acc

    groups = d.c // 8
    depthwise(d, main, side, columns, False, start, store, 0, groups)
    mlp(d, pre, cot, columns, lift_t, lift, drop_t, dmain, big_lift, big_drop, gain_acc, shift_acc)
    finish = ex(1, dmain, dside)
    sums.start_pair(big_lift, big_drop)
    lane = lanes((d.c, d.cols))
    small_cols[...] = jnp.zeros_like(small_cols)
    small_cols[: d.c, :] = jnp.where(
        lane == taps_n + 1,
        jnp.sum(gain_acc[...], axis=1, keepdims=True),
        jnp.where(lane == taps_n + 2, jnp.sum(shift_acc[...], axis=1, keepdims=True), 0.0),
    )
    kernel_grads(d, main, side, dmain, small_cols)
    lane = lanes((wide, d.cols))
    for b in range(blocks):
        column = big_lift[b * wide : (b + 1) * wide, d.c : d.c + 1]
        small_cols[...] = jnp.where(lane == taps_n + 3 + b, column, small_cols[...])
    for h in range(2):
        turned = small_cols[h * 128 : h * 128 + 128, :].T
        for i in range(8):
            sums.small[h * 8 + i] = turned[i * 8 : i * 8 + 8]
    sums.start_chips()
    sums.start_small()
    finish()

    def start_back(g, at):
        return jnp.zeros((d.rows, 8, d.cols), F32)

    third = groups // 3
    depthwise(d, dmain, dside, columns, True, start_back, store, 0, third)
    sums.start_gather()
    sums.start_small_gather()
    depthwise(d, dmain, dside, columns, True, start_back, store, third, 2 * third)
    sums.start_back()
    depthwise(d, dmain, dside, columns, True, start_back, store, 2 * third, groups)
    for r in range(d.rows):
        flat[pl.ds(r, d.c, stride=d.rows), :] = mask * (pre[r] + cot[r].astype(F32))
    out[0] = flat[...].reshape(d.c, d.rows, d.cols).astype(BF16)
    small = sums.finish_small()
    for h, (lo, hi) in enumerate(((0, 128), (128, d.c))):
        base = h * 64
        out_taps[:, lo:hi] = small[base : base + taps_n, 0 : hi - lo]
        for k, one in enumerate((out_offset, out_gain, out_shift)):
            one[:, lo:hi] = small[base + taps_n + k : base + taps_n + k + 1, 0 : hi - lo]
        for b in range(blocks):
            out_bias[:, b * wide + h * 128 : b * wide + h * 128 + 128] = small[
                base + taps_n + 3 + b : base + taps_n + 4 + b
            ]
    sums.finish(out_lift, out_drop)


def body(
    n,
    saved_input,
    tile_scale,
    ocean_tiles,
    upstream,
    kernel_taps,
    kernel_offset,
    norm_gain,
    norm_shift,
    lift_weight,
    lift_bias,
    drop_weight,
):
    channels, rows, cols = saved_input.shape[1:]
    hidden = lift_weight.shape[1]
    taps_n = kernel_taps.shape[0]
    d = Dims(n, channels, rows, cols, math.isqrt(taps_n), hidden)
    vmem = pl.BlockSpec(memory_space=pltpu.VMEM)
    grid3 = (d.ext, channels, cols)
    factor = 1.0 / math.sqrt(n * rows * cols)
    chips = d.group // 2
    chunk = hidden // d.group
    dma = pltpu.SemaphoreType.DMA
    out, *grads = pl.pallas_call(
        functools.partial(kernel, d, factor),
        out_shape=(
            jax.ShapeDtypeStruct((1, channels, rows, cols), BF16),
            jax.ShapeDtypeStruct((taps_n, channels), F32),
            jax.ShapeDtypeStruct((1, channels), F32),
            jax.ShapeDtypeStruct((1, channels), F32),
            jax.ShapeDtypeStruct((1, channels), F32),
            jax.ShapeDtypeStruct((channels, hidden), F32),
            jax.ShapeDtypeStruct((1, hidden), F32),
            jax.ShapeDtypeStruct((channels, hidden), F32),
        ),
        in_specs=[vmem] * 11,
        out_specs=(vmem,) * 8,
        scratch_shapes=[
            pltpu.VMEM((channels * rows, cols), F32),
            pltpu.VMEM(grid3, F32),
            pltpu.VMEM(grid3, F32),
            pltpu.VMEM(grid3, F32),
            pltpu.VMEM(grid3, F32),
            pltpu.VMEM((rows, channels, cols), BF16),
            pltpu.VMEM((rows, channels, cols), F32),
            pltpu.VMEM((2, 2, d.reach, channels, cols), BF16),
            pltpu.VMEM((2, 2, d.reach, channels, cols), BF16),
            pltpu.VMEM((2, channels, cols), BF16),
            pltpu.VMEM((2, 2, channels, cols), BF16),
            pltpu.VMEM((2, 2, 2, channels, cols), BF16),
            pltpu.VMEM((channels, cols), F32),
            pltpu.VMEM((channels, cols), F32),
            dma((2, 8)),
            dma((2, 8)),
            pltpu.VMEM((256, 128), F32),
            pltpu.VMEM((hidden, channels), BF16),
            pltpu.VMEM((hidden, channels), BF16),
            pltpu.VMEM((hidden, 256), F32),
            pltpu.VMEM((hidden, 256), F32),
            pltpu.VMEM((256, 128), F32),
            pltpu.VMEM((2, chips, chunk, 384), BF16),
            pltpu.VMEM((chips, chunk, 384), BF16),
            pltpu.VMEM((chips, chunk, 384), BF16),
            pltpu.VMEM((chips - 1, chunk, 384), BF16),
            pltpu.VMEM((2, chips, chunk, 384), BF16),
            pltpu.VMEM((d.group, 8, 128), F32),
            pltpu.VMEM((d.group - 1, 8, 128), F32),
            pltpu.VMEM((d.group, 8, 128), F32),
            dma((2,)),
            dma((2, chips)),
            dma((2, chips)),
            dma((2,)),
            dma((2, d.group)),
            dma((2, d.group)),
        ],
        compiler_params=pltpu.CompilerParams(
            collective_id=0, has_side_effects=True, vmem_limit_bytes=56 * 1024 * 1024
        ),
        name="block_backward",
    )(
        saved_input,
        tile_scale,
        ocean_tiles,
        upstream,
        kernel_taps,
        kernel_offset[None],
        norm_gain[None],
        norm_shift[None],
        lift_weight,
        lift_bias[None],
        drop_weight.T,
    )
    if n != d.group:
        across = [[i + d.group * k for k in range(n // d.group)] for i in range(d.group)]
        grads = lax.psum(grads, "lon", axis_index_groups=across)
    g_taps, g_offset, g_gain, g_shift, g_lift, g_bias, g_drop = grads
    return (out, g_taps, g_offset[0], g_gain[0], g_shift[0], g_lift, g_bias.reshape(-1), g_drop.T)


def solution(mesh):
    return jax.shard_map(
        functools.partial(body, mesh.shape["lon"]),
        mesh=mesh,
        in_specs=(
            P(("ens", "lon"), None, None, None),
            P(("ens", "lon"), None, None),
            P(("ens", "lon"), None),
            P(("ens", "lon"), None, None, None),
            P(),
            P(),
            P(),
            P(),
            P(),
            P(),
            P(),
        ),
        out_specs=(
            P(("ens", "lon"), None, None, None),
            P("ens", None),
            P("ens"),
            P("ens"),
            P("ens"),
            P("ens", None),
            P("ens"),
            P("ens", None),
        ),
        check_vma=False,
    )
```
